32 devices in a mesh: seq: 4 (over z), grp: 8 (over y, x, core).
Axes of the slice: x: 2, y: 2, z: 4, core: 2. Of those that a mesh axis runs over, the one named last changes fastest.
Arguments:
- qkv: bfloat16 [8192, 3, 2048], P(('seq', 'grp')), may hold values from -6 to 6
- cluster_lists: int32 [16, 8, 1024], P('seq', 'grp'), may hold values from 0 to 8191, as said below
- w_out: bfloat16 [2048, 2048], replicated, may hold values from -0.125 to 0.125
- norm_gain: bfloat16 [2048], replicated, may hold values from 0.099609375 to 1.8984375
- router: bfloat16 [2048, 32], replicated, may hold values from -0.125 to 0.125
- expert_lists: int32 [32, 512], replicated, may hold values from 0 to 8191, as said below
- w_gate: bfloat16 [32, 2048, 768], P(('seq', 'grp')), may hold values from -0.125 to 0.125
- w_up: bfloat16 [32, 2048, 768], P(('seq', 'grp')), may hold values from -0.125 to 0.125
- w_down: bfloat16 [32, 768, 2048], P(('seq', 'grp')), may hold values from -0.21875 to 0.21875
Outputs:
- layer_out: bfloat16 [8192, 2048], P(('seq', 'grp'))
The draws below stay inside these ranges and needn't reach their ends.
Inputs may be any that keep to these rules, and one draw needn't show every extreme that they name: `cluster_lists`: within each head the 8 lists are disjoint, each ascending, and together hold every one of the 8192 tokens once. Of the 256 tokens of an aligned block, one list holds at most 48, and for every head some list holds exactly 48. `expert_lists`: each list is ascending with distinct rows. Of the 256 rows of an aligned block, one list holds at most 24, and some list holds exactly 24.
All inputs are finite; a program needn't handle non-finite values.
Results may differ from the reference program's by a relative error of at most 0.019.
Values may be sent and summed in bfloat16 or wider, within the bound.
A program may use at most 128 MiB of HBM per device.

```python
import jax
import jax.numpy as jnp
from jax import lax

HEADS = 16
HEAD_DIM = 128
D = 2048
EXPERT_HIDDEN = 768
ECHOOSE = 512
C = 1024
CLUSTERS = 8
TOKENS = 8192
ROWS = 256
HD = 2048
EXPERTS = 32


def draw_qkv(key, part):
    values = jnp.clip(jax.random.normal(key, (TOKENS, 3, HEADS * HEAD_DIM), jnp.float32), -4.0, 4.0)
    return values.astype(jnp.bfloat16)


def draw_cluster_lists(key, part):
    blocks = TOKENS // ROWS
    mean_load = ROWS // CLUSTERS

    def one_head(head_key):
        key_shift, key_heavy, key_mix = jax.random.split(head_key, 3)
        loads_base = jnp.where(jnp.arange(CLUSTERS, dtype=jnp.int32) < CLUSTERS // 2, mean_load // 2, 3 * mean_load // 2)
        loads_base = jax.random.permutation(key_heavy, loads_base)
        shifts = jax.random.permutation(key_shift, blocks) % CLUSTERS
        counts = loads_base[(jnp.arange(CLUSTERS, dtype=jnp.int32)[None, :] + shifts[:, None]) % CLUSTERS]
        bounds = jnp.cumsum(counts, axis=1)
        offsets = jnp.arange(ROWS, dtype=jnp.int32)
        labels = jnp.sum((offsets[None, :, None] >= bounds[:, None, :]).astype(jnp.int32), axis=2)
        labels = jax.random.permutation(key_mix, labels, axis=1, independent=True)
        assign = labels.reshape(TOKENS)
        order = jnp.argsort(assign * TOKENS + jnp.arange(TOKENS, dtype=jnp.int32), stable=True)
        return order.reshape(CLUSTERS, C).astype(jnp.int32)
    return jax.vmap(one_head)(jax.random.split(jax.random.fold_in(key, 11), HEADS))


def draw_expert_lists(key, part):
    blocks = TOKENS // ROWS
    mean_load = ECHOOSE // EXPERTS
    key_heavy, key_shift, key_pick = jax.random.split(jax.random.fold_in(key, 13), 3)
    loads_base = jnp.where(jnp.arange(EXPERTS, dtype=jnp.int32) < EXPERTS // 2, mean_load // 2, 3 * mean_load // 2)
    loads_base = jax.random.permutation(key_heavy, loads_base)
    shifts = jax.random.permutation(key_shift, blocks)
    counts = loads_base[(jnp.arange(EXPERTS, dtype=jnp.int32)[None, :] + shifts[:, None]) % EXPERTS]
    ranks = jnp.broadcast_to(jnp.arange(ROWS, dtype=jnp.int32), (EXPERTS, blocks, ROWS))
    ranks = jax.random.permutation(key_pick, ranks, axis=2, independent=True)
    chosen = (ranks < counts.T[:, :, None]).reshape(EXPERTS, TOKENS)
    order_key = jnp.where(chosen, 0, 1) * TOKENS + jnp.arange(TOKENS, dtype=jnp.int32)[None, :]
    order = jnp.argsort(order_key, axis=1, stable=True)
    return order[:, :ECHOOSE].astype(jnp.int32)


def steps_of(stream_key, shape, cuts, smallest, high):
    loudness = 1.0
    for position, shards_of in cuts:
        steps = jax.random.uniform(jax.random.fold_in(jax.random.fold_in(stream_key, 6), position), (shards_of,), jnp.float32, smallest / len(cuts), high / len(cuts))
        loudness = loudness * jnp.repeat(jnp.exp(steps), shape[position] // shards_of).reshape((-1,) + (1,) * (len(shape) - 1 - position))
    return loudness


def bell_draw(own_key, dims, spread, bound, pieces=(), kind=jnp.bfloat16):
    drawn = spread * jax.random.normal(own_key, dims, jnp.float32)
    if pieces:
        drawn = drawn * steps_of(own_key, dims, pieces, -0.22, 0.18)
    return jnp.clip(drawn, -bound, bound).astype(kind)


def setup_inputs(seed: int = 0) -> dict:
    key_list = jax.random.split(jax.random.key(seed), 10)
    return {
        "qkv": draw_qkv(jax.random.fold_in(key_list[9], 71), 0),
        "cluster_lists": draw_cluster_lists(jax.random.fold_in(key_list[9], 71), 0),
        "w_out": bell_draw(key_list[2], (HD, D), HD ** -0.5, 0.125),
        "norm_gain": jnp.clip(1.0 + 0.18 * jax.random.normal(key_list[3], (D,), jnp.float32), 0.099609375, 1.8984375).astype(jnp.bfloat16),
        "router": bell_draw(key_list[4], (D, EXPERTS), D ** -0.5, 0.125),
        "expert_lists": draw_expert_lists(jax.random.fold_in(key_list[9], 71), 0),
        "w_gate": bell_draw(key_list[6], (EXPERTS, D, EXPERT_HIDDEN), D ** -0.5, 0.125, ((0, 32),)),
        "w_up": bell_draw(key_list[7], (EXPERTS, D, EXPERT_HIDDEN), D ** -0.5, 0.125, ((0, 32),)),
        "w_down": bell_draw(key_list[8], (EXPERTS, EXPERT_HIDDEN, D), EXPERT_HIDDEN ** -0.5, 0.21875, ((0, 32),)),
    }


def cluster_attention(packed):
    queries = packed[:, 0, :]
    keys_all = packed[:, 1, :]
    values_all = packed[:, 2, :]
    scores = jnp.dot(queries, keys_all.T, preferred_element_type=jnp.float32) * HEAD_DIM ** (-0.5)
    positions = jnp.arange(C, dtype=jnp.int32)
    allowed = positions[:, None] >= positions[None, :]
    scores = jnp.where(allowed, scores, -jnp.inf)
    top_score = lax.optimization_barrier(jnp.max(scores, axis=1, keepdims=True))
    exp_scores = jnp.exp(scores - top_score)
    weights = exp_scores.astype(jnp.bfloat16)
    totals = lax.optimization_barrier(jnp.sum(exp_scores, axis=1, keepdims=True))
    return (jnp.dot(weights, values_all, preferred_element_type=jnp.float32) / totals).astype(jnp.bfloat16)

def reference(qkv, cluster_lists, w_out, norm_gain, router, expert_lists, w_gate, w_up, w_down):
    by_head = qkv.reshape(TOKENS, 3, HEADS, HEAD_DIM).transpose(2, 0, 1, 3)

    def one_head(operands):
        head_rows, head_lists = operands

        def one_cluster(members):
            return cluster_attention(head_rows[members])
        outputs = lax.map(one_cluster, head_lists)
        empty = jnp.zeros((TOKENS, HEAD_DIM), jnp.bfloat16)
        return empty.at[head_lists.reshape(-1)].add(outputs.reshape(-1, HEAD_DIM))
    attended = lax.map(one_head, (by_head, cluster_lists))
    attended = attended.transpose(1, 0, 2).reshape(TOKENS, HEADS * HEAD_DIM)
    mixed = jnp.dot(attended, w_out, preferred_element_type=jnp.float32).astype(jnp.bfloat16)
    wide = mixed.astype(jnp.float32)
    mean_square = lax.optimization_barrier(jnp.mean(wide * wide, axis=1, keepdims=True))
    normed = (wide * lax.rsqrt(mean_square + 1e-06) * norm_gain.astype(jnp.float32)).astype(jnp.bfloat16)
    gates = jax.nn.sigmoid(jnp.dot(normed, router, preferred_element_type=jnp.float32))

    def one_expert(operands):
        chosen, gate_w, up_w, down_w = operands
        rows_in = normed[chosen]
        gate_part = jnp.dot(rows_in, gate_w, preferred_element_type=jnp.float32)
        up_part = jnp.dot(rows_in, up_w, preferred_element_type=jnp.float32)
        hidden = (jax.nn.silu(gate_part) * up_part).astype(jnp.bfloat16)
        return jnp.dot(hidden, down_w, preferred_element_type=jnp.float32).astype(jnp.bfloat16)
    results = lax.map(one_expert, (expert_lists, w_gate, w_up, w_down))
    expert_ids = jnp.arange(EXPERTS, dtype=jnp.int32)[:, None]
    weights = gates[expert_lists, expert_ids]
    terms = (weights[:, :, None] * results.astype(jnp.float32)).reshape(-1, D)
    combined = jnp.zeros((TOKENS, D), jnp.float32).at[expert_lists.reshape(-1)].add(terms)
    return (wide + combined).astype(jnp.bfloat16)
```

```python
import functools

import jax
import jax.numpy as jnp
from jax import lax
from jax.experimental import pallas as pl
from jax.experimental.pallas import tpu as pltpu
from jax.sharding import PartitionSpec as P

MESH = pl.DeviceIdType.MESH
F32 = jnp.float32
BF16 = jnp.bfloat16


def round_up(value, step):
    return (value + step - 1) // step * step


def select_matrix(code, slots):
    lists, rows = code.shape
    slot_iota = lax.broadcasted_iota(jnp.int32, (slots, rows), 0).astype(F32)
    parts = [
        jnp.where(code[g : g + 1, :] == slot_iota, 1.0, 0.0).astype(BF16) for g in range(lists)
    ]
    return jnp.concatenate(parts, axis=0)


def attention_kernel(
    S, G, H, R, C, dh, scale,
    x_ref, code_ref, bias_ref, out_ref,
    zin, psend, arr, osend, oarr, zback,
    zs_send, zs_recv, ps_send, ps_recv, os_send, os_recv, bs_send, bs_recv,
):
    s = lax.axis_index("seq")
    g = lax.axis_index("grp")

    barrier = pltpu.get_barrier_semaphore()
    for d in range(1, S):
        pl.semaphore_signal(barrier, inc=1, device_id=(lax.rem(s + d, S), g), device_id_type=MESH)
    for d in range(1, G):
        pl.semaphore_signal(barrier, inc=1, device_id=(s, lax.rem(g + d, G)), device_id_type=MESH)
    pl.semaphore_wait(barrier, S + G - 2)

    def z_copy(j, d):
        to = lax.rem(s + d, S)
        return pltpu.make_async_remote_copy(
            src_ref=x_ref.at[to, j], dst_ref=zin.at[j, s],
            send_sem=zs_send.at[j, d], recv_sem=zs_recv.at[j, s],
            device_id=(to, g), device_id_type=MESH,
        )

    def z_own(j):
        return pltpu.make_async_copy(x_ref.at[s, j], zin.at[j, s], zs_recv.at[j, s])

    def z_arrival(j, src):
        return pltpu.make_async_copy(zin.at[j, src], zin.at[j, src], zs_recv.at[j, src])

    def p_copy(j, d):
        to = lax.rem(g + d, G)
        return pltpu.make_async_remote_copy(
            src_ref=psend.at[j, :, to], dst_ref=arr.at[j, :, g],
            send_sem=ps_send.at[j, d], recv_sem=ps_recv.at[j, g],
            device_id=(s, to), device_id_type=MESH,
        )

    def p_own(j):
        return pltpu.make_async_copy(psend.at[j, :, g], arr.at[j, :, g], ps_recv.at[j, g])

    def p_arrival(j, src):
        return pltpu.make_async_copy(arr.at[j, :, src], arr.at[j, :, src], ps_recv.at[j, src])

    def o_copy(j, d):
        to = lax.rem(g + d, G)
        return pltpu.make_async_remote_copy(
            src_ref=osend.at[j, :, to], dst_ref=oarr.at[j, :, g],
            send_sem=os_send.at[j, d], recv_sem=os_recv.at[j, g],
            device_id=(s, to), device_id_type=MESH,
        )

    def o_own(j):
        return pltpu.make_async_copy(osend.at[j, :, g], oarr.at[j, :, g], os_recv.at[j, g])

    def o_arrival(j, src):
        return pltpu.make_async_copy(oarr.at[j, :, src], oarr.at[j, :, src], os_recv.at[j, src])

    def columns(owner, j):
        return pl.ds(pl.multiple_of((owner * H + j) * dh, dh), dh)

    def b_copy(j, d):
        to = lax.rem(s + d, S)
        return pltpu.make_async_remote_copy(
            src_ref=zback.at[j, to], dst_ref=out_ref.at[:, columns(s, j)],
            send_sem=bs_send.at[j, d], recv_sem=bs_recv.at[j, s],
            device_id=(to, g), device_id_type=MESH,
        )

    def b_own(j):
        return pltpu.make_async_copy(
            zback.at[j, s], out_ref.at[:, columns(s, j)], bs_recv.at[j, s]
        )

    def b_arrival(j, src):
        where = out_ref.at[:, columns(src, j)]
        return pltpu.make_async_copy(where, where, bs_recv.at[j, src])

    def z_start(j):
        for d in range(1, S):
            z_copy(j, d).start()
        z_own(j).start()

    z_start(0)
    if H > 1:
        z_start(1)

    def route(j):
        for src in range(S):
            z_arrival(j, src).wait()

        @pl.when(j + 2 < H)
        def _():
            z_start(j + 2)

        for z in range(S):
            sel = select_matrix(code_ref[j, z], C)
            picked = jnp.dot(sel, zin[j, z], preferred_element_type=F32)
            psend[j, z] = picked.astype(BF16).reshape(G, C, 3 * dh)
        for d in range(1, G):
            p_copy(j, d).start()
        p_own(j).start()

    def attend(j):
        for src in range(G):
            p_arrival(j, src).wait()
        n = G * C
        causal = lax.broadcasted_iota(jnp.int32, (n, n), 0) >= lax.broadcasted_iota(
            jnp.int32, (n, n), 1
        )
        for z in range(S):
            q = arr[j, z, :, :, 0:dh].reshape(n, dh)
            scores = []
            for y in range(z + 1):
                k = arr[j, y, :, :, dh : 2 * dh].reshape(n, dh)
                part = lax.dot_general(
                    q, k, (((1,), (1,)), ((), ())), preferred_element_type=F32
                )
                part = part * scale + bias_ref[j, y]
                if y == z:
                    part = jnp.where(causal, part, -1e30)
                scores.append(part)
            top = functools.reduce(
                jnp.maximum, [jnp.max(part, axis=1, keepdims=True) for part in scores]
            )
            total = jnp.zeros((n, 1), F32)
            acc = jnp.zeros((n, dh), F32)
            for y in range(z + 1):
                e = jnp.exp(scores[y] - top)
                total = total + jnp.sum(e, axis=1, keepdims=True)
                v = arr[j, y, :, :, 2 * dh : 3 * dh].reshape(n, dh)
                acc = acc + jnp.dot(e.astype(BF16), v, preferred_element_type=F32)
            osend[j, z] = (acc / total).astype(BF16).reshape(G, C, dh)
        for d in range(1, G):
            o_copy(j, d).start()
        o_own(j).start()

    def give_back(j):
        for src in range(G):
            o_arrival(j, src).wait()
        for z in range(S):
            sel = select_matrix(code_ref[j, z], C)
            rows = lax.dot_general(
                sel, oarr[j, z].reshape(G * C, dh), (((0,), (0,)), ((), ())),
                preferred_element_type=F32,
            )
            zback[j, z] = rows.astype(BF16)
        for d in range(1, S):
            b_copy(j, d).start()
        b_own(j).start()

    @pl.loop(0, H + 2)
    def _(t):
        @pl.when(t < H)
        def _():
            route(t)

        @pl.when((t >= 1) & (t <= H))
        def _():
            attend(t - 1)

        @pl.when(t >= 2)
        def _():
            give_back(t - 2)

    @pl.loop(0, H)
    def _(j):
        for src in range(S):
            b_arrival(j, src).wait()
        for d in range(1, S):
            z_copy(j, d).wait_send()
            b_copy(j, d).wait_send()
        for d in range(1, G):
            p_copy(j, d).wait_send()
            o_copy(j, d).wait_send()


def cluster_attention(x, code, bias, S, G, H, R, C, dh):
    W = 3 * dh
    vmem = pl.BlockSpec(memory_space=pltpu.VMEM)
    pairs = H * S * G * C * G * C * (S + 1) // 2
    return pl.pallas_call(
        functools.partial(attention_kernel, S, G, H, R, C, dh, dh ** (-0.5)),
        out_shape=jax.ShapeDtypeStruct((R, S * H * dh), BF16),
        in_specs=[pl.BlockSpec(memory_space=pl.ANY), vmem, vmem],
        out_specs=vmem,
        scratch_shapes=[
            pltpu.VMEM((H, S, R, W), BF16),
            pltpu.VMEM((H, S, G, C, W), BF16),
            pltpu.VMEM((H, S, G, C, W), BF16),
            pltpu.VMEM((H, S, G, C, dh), BF16),
            pltpu.VMEM((H, S, G, C, dh), BF16),
            pltpu.VMEM((H, S, R, dh), BF16),
            pltpu.SemaphoreType.DMA((H, S)),
            pltpu.SemaphoreType.DMA((H, S)),
            pltpu.SemaphoreType.DMA((H, G)),
            pltpu.SemaphoreType.DMA((H, G)),
            pltpu.SemaphoreType.DMA((H, G)),
            pltpu.SemaphoreType.DMA((H, G)),
            pltpu.SemaphoreType.DMA((H, S)),
            pltpu.SemaphoreType.DMA((H, S)),
        ],
        compiler_params=pltpu.CompilerParams(
            collective_id=0, has_side_effects=True, vmem_limit_bytes=52 * 1024 * 1024
        ),
        cost_estimate=pl.CostEstimate(
            flops=4 * pairs * dh, bytes_accessed=2 * H * S * R * W, transcendentals=pairs
        ),
    )(x, code, bias)


def expert_mlp(rows_in, gate_w, up_w, down_w):
    gate_part = jnp.dot(rows_in, gate_w, preferred_element_type=F32)
    up_part = jnp.dot(rows_in, up_w, preferred_element_type=F32)
    hidden = (jax.nn.silu(gate_part) * up_part).astype(BF16)
    return jnp.dot(hidden, down_w, preferred_element_type=F32).astype(BF16)


def slot_codes(mask):
    rows = mask.shape[-1]
    before = jnp.triu(jnp.ones((rows, rows), BF16), 1)
    ranks = jnp.einsum("...r,rq->...q", mask.astype(BF16), before, preferred_element_type=F32)
    return jnp.where(mask > 0, ranks, -1.0)


def shards(qkv, cluster_lists, w_out, norm_gain, router, expert_lists, w_gate, w_up, w_down):
    R = qkv.shape[0]
    S = lax.axis_size("seq")
    G = lax.axis_size("grp")
    devices = S * G
    H = cluster_lists.shape[0]
    dh = qkv.shape[2] // (H * S)
    my_index = lax.axis_index("seq") * G + lax.axis_index("grp")
    C = round_up(3 * (R // G) // 2, 16)

    x = qkv.reshape(R, 3, S * H, dh).transpose(2, 0, 1, 3).reshape(S, H, R, 3 * dh)
    members = cluster_lists[:, 0, :]
    lanes = 128
    high = (
        (members // lanes)[:, None, :] == jnp.arange(devices * R // lanes, dtype=jnp.int32)[:, None]
    )
    low = (members % lanes)[:, :, None] == jnp.arange(lanes, dtype=jnp.int32)
    mask = jnp.einsum(
        "hip,hpl->hil", high.astype(BF16), low.astype(BF16), preferred_element_type=F32
    ).reshape(H, S, G, R)
    counts = jnp.sum(mask, axis=3)
    slots = jnp.arange(C, dtype=F32)
    bias = jnp.where(slots < counts[..., None], 0.0, -1e30).reshape(H, S, 1, G * C)
    asked = lax.all_to_all(mask.astype(BF16), "grp", split_axis=2, concat_axis=2, tiled=True)
    code = slot_codes(asked)

    attended = cluster_attention(x, code, bias, S, G, H, R, C, dh)
    mixed = jnp.dot(attended, w_out, preferred_element_type=F32).astype(BF16)
    wide = mixed.astype(F32)
    mean_square = jnp.mean(wide * wide, axis=1, keepdims=True)
    normed = (wide * lax.rsqrt(mean_square + 1e-06) * norm_gain.astype(F32)).astype(BF16)
    gates = jax.nn.sigmoid(jnp.dot(normed, router, preferred_element_type=F32))

    E, chosen_len = expert_lists.shape
    cap = 3 * (chosen_len // devices) // 2
    row_iota = jnp.arange(R, dtype=jnp.int32)
    here = expert_lists - my_index * R
    expert_mask = jnp.sum((here[:, :, None] == row_iota).astype(F32), axis=1)
    expert_code = slot_codes(expert_mask)
    match = expert_code[:, None, :] == jnp.arange(cap, dtype=F32)[None, :, None]
    outgoing = jnp.einsum(
        "ecr,rd->ecd", match.astype(BF16), normed, preferred_element_type=F32
    ).astype(BF16)
    incoming = lax.all_to_all(outgoing, ("seq", "grp"), split_axis=0, concat_axis=0, tiled=True)
    back = expert_mlp(
        incoming.reshape(devices * cap, -1), w_gate[0], w_up[0], w_down[0]
    ).reshape(devices, cap, -1)
    results = lax.all_to_all(back, ("seq", "grp"), split_axis=0, concat_axis=0, tiled=True)
    share = jnp.where(match, gates.T[:, None, :], 0.0).astype(BF16)
    combined = jnp.einsum("ecr,ecd->rd", share, results, preferred_element_type=F32)
    return (wide + combined).astype(BF16)


def solution(mesh):
    return jax.shard_map(
        shards,
        mesh=mesh,
        in_specs=(
            P(("seq", "grp"), None, None),
            P("seq", "grp", None),
            P(),
            P(),
            P(),
            P(),
            P(("seq", "grp"), None, None),
            P(("seq", "grp"), None, None),
            P(("seq", "grp"), None, None),
        ),
        out_specs=P(("seq", "grp"), None),
        check_vma=False,
    )
```

```python
import functools

import jax
import jax.numpy as jnp
from jax import lax
from jax.experimental import pallas as pl
from jax.experimental.pallas import tpu as pltpu
from jax.sharding import PartitionSpec as P

MESH = pl.DeviceIdType.MESH
F32 = jnp.float32
BF16 = jnp.bfloat16


def round_up(value, step):
    return (value + step - 1) // step * step


def select_matrix(code, slots):
    lists, rows = code.shape
    slot_iota = lax.broadcasted_iota(jnp.int32, (slots, rows), 0).astype(F32)
    parts = [
        jnp.where(code[g : g + 1, :] == slot_iota, 1.0, 0.0).astype(BF16) for g in range(lists)
    ]
    return jnp.concatenate(parts, axis=0)


def attention_kernel(
    S, G, H, R, C, dh, scale,
    x_ref, code_ref, bias_ref, out_ref,
    zin, psend, arr, osend, oarr, zback,
    zs_send, zs_recv, ps_send, ps_recv, os_send, os_recv, bs_send, bs_recv,
):
    s = lax.axis_index("seq")
    g = lax.axis_index("grp")

    barrier = pltpu.get_barrier_semaphore()
    for d in range(1, S):
        pl.semaphore_signal(barrier, inc=1, device_id=(lax.rem(s + d, S), g), device_id_type=MESH)
    for d in range(1, G):
        pl.semaphore_signal(barrier, inc=1, device_id=(s, lax.rem(g + d, G)), device_id_type=MESH)
    pl.semaphore_wait(barrier, S + G - 2)

    def head_part(owner, j, k):
        return x_ref.at[:, pl.ds(pl.multiple_of(((k * S + owner) * H + j) * dh, dh), dh)]

    def z_copy(j, d, k):
        to = lax.rem(s + d, S)
        return pltpu.make_async_remote_copy(
            src_ref=head_part(to, j, k), dst_ref=zin.at[j, s, :, k * dh : (k + 1) * dh],
            send_sem=zs_send.at[j, d, k], recv_sem=zs_recv.at[j, s],
            device_id=(to, g), device_id_type=MESH,
        )

    def z_own(j, k):
        return pltpu.make_async_copy(
            head_part(s, j, k), zin.at[j, s, :, k * dh : (k + 1) * dh], zs_recv.at[j, s]
        )

    def z_arrival(j, src):
        return pltpu.make_async_copy(zin.at[j, src], zin.at[j, src], zs_recv.at[j, src])

    def p_copy(j, d):
        to = lax.rem(g + d, G)
        return pltpu.make_async_remote_copy(
            src_ref=psend.at[j, :, to], dst_ref=arr.at[j, :, g],
            send_sem=ps_send.at[j, d], recv_sem=ps_recv.at[j, g],
            device_id=(s, to), device_id_type=MESH,
        )

    def p_own(j):
        return pltpu.make_async_copy(psend.at[j, :, g], arr.at[j, :, g], ps_recv.at[j, g])

    def p_arrival(j, src):
        return pltpu.make_async_copy(arr.at[j, :, src], arr.at[j, :, src], ps_recv.at[j, src])

    def o_copy(j, d):
        to = lax.rem(g + d, G)
        return pltpu.make_async_remote_copy(
            src_ref=osend.at[j, :, to], dst_ref=oarr.at[j, :, g],
            send_sem=os_send.at[j, d], recv_sem=os_recv.at[j, g],
            device_id=(s, to), device_id_type=MESH,
        )

    def o_own(j):
        return pltpu.make_async_copy(osend.at[j, :, g], oarr.at[j, :, g], os_recv.at[j, g])

    def o_arrival(j, src):
        return pltpu.make_async_copy(oarr.at[j, :, src], oarr.at[j, :, src], os_recv.at[j, src])

    def columns(owner, j):
        return pl.ds(pl.multiple_of((owner * H + j) * dh, dh), dh)

    def b_copy(j, d):
        to = lax.rem(s + d, S)
        return pltpu.make_async_remote_copy(
            src_ref=zback.at[j, to], dst_ref=out_ref.at[:, columns(s, j)],
            send_sem=bs_send.at[j, d], recv_sem=bs_recv.at[j, s],
            device_id=(to, g), device_id_type=MESH,
        )

    def b_own(j):
        return pltpu.make_async_copy(
            zback.at[j, s], out_ref.at[:, columns(s, j)], bs_recv.at[j, s]
        )

    def b_arrival(j, src):
        where = out_ref.at[:, columns(src, j)]
        return pltpu.make_async_copy(where, where, bs_recv.at[j, src])

    def z_start(j):
        for k in range(3):
            for d in range(1, S):
                z_copy(j, d, k).start()
            z_own(j, k).start()

    z_start(0)
    if H > 1:
        z_start(1)

    def route(j):
        for src in range(S):
            z_arrival(j, src).wait()

        @pl.when(j + 2 < H)
        def _():
            z_start(j + 2)

        for z in range(S):
            sel = select_matrix(code_ref[j, z], C)
            picked = jnp.dot(sel, zin[j, z], preferred_element_type=F32)
            psend[j, z] = picked.astype(BF16).reshape(G, C, 3 * dh)
        for d in range(1, G):
            p_copy(j, d).start()
        p_own(j).start()

    def attend(j):
        for src in range(G):
            p_arrival(j, src).wait()
        n = G * C
        causal = lax.broadcasted_iota(jnp.int32, (n, n), 0) >= lax.broadcasted_iota(
            jnp.int32, (n, n), 1
        )
        for z in range(S):
            q = arr[j, z, :, :, 0:dh].reshape(n, dh)
            scores = []
            for y in range(z + 1):
                k = arr[j, y, :, :, dh : 2 * dh].reshape(n, dh)
                part = lax.dot_general(
                    q, k, (((1,), (1,)), ((), ())), preferred_element_type=F32
                )
                part = part * scale + bias_ref[j, y]
                if y == z:
                    part = jnp.where(causal, part, -1e30)
                scores.append(part)
            top = functools.reduce(
                jnp.maximum, [jnp.max(part, axis=1, keepdims=True) for part in scores]
            )
            total = jnp.zeros((n, 1), F32)
            acc = jnp.zeros((n, dh), F32)
            for y in range(z + 1):
                e = jnp.exp(scores[y] - top)
                total = total + jnp.sum(e, axis=1, keepdims=True)
                v = arr[j, y, :, :, 2 * dh : 3 * dh].reshape(n, dh)
                acc = acc + jnp.dot(e.astype(BF16), v, preferred_element_type=F32)
            osend[j, z] = (acc / total).astype(BF16).reshape(G, C, dh)
        for d in range(1, G):
            o_copy(j, d).start()
        o_own(j).start()

    def give_back(j):
        for src in range(G):
            o_arrival(j, src).wait()
        for z in range(S):
            sel = select_matrix(code_ref[j, z], C)
            rows = lax.dot_general(
                sel, oarr[j, z].reshape(G * C, dh), (((0,), (0,)), ((), ())),
                preferred_element_type=F32,
            )
            zback[j, z] = rows.astype(BF16)
        for d in range(1, S):
            b_copy(j, d).start()
        b_own(j).start()

    @pl.loop(0, H + 2)
    def _(t):
        @pl.when(t < H)
        def _():
            route(t)

        @pl.when((t >= 1) & (t <= H))
        def _():
            attend(t - 1)

        @pl.when(t >= 2)
        def _():
            give_back(t - 2)

    @pl.loop(0, H)
    def _(j):
        for src in range(S):
            b_arrival(j, src).wait()
        for d in range(1, S):
            for k in range(3):
                z_copy(j, d, k).wait_send()
            b_copy(j, d).wait_send()
        for d in range(1, G):
            p_copy(j, d).wait_send()
            o_copy(j, d).wait_send()


def cluster_attention(x, code, bias, S, G, H, R, C, dh):
    W = 3 * dh
    vmem = pl.BlockSpec(memory_space=pltpu.VMEM)
    pairs = H * S * G * C * G * C * (S + 1) // 2
    return pl.pallas_call(
        functools.partial(attention_kernel, S, G, H, R, C, dh, dh ** (-0.5)),
        out_shape=jax.ShapeDtypeStruct((R, S * H * dh), BF16),
        in_specs=[pl.BlockSpec(memory_space=pl.ANY), vmem, vmem],
        out_specs=vmem,
        scratch_shapes=[
            pltpu.VMEM((H, S, R, W), BF16),
            pltpu.VMEM((H, S, G, C, W), BF16),
            pltpu.VMEM((H, S, G, C, W), BF16),
            pltpu.VMEM((H, S, G, C, dh), BF16),
            pltpu.VMEM((H, S, G, C, dh), BF16),
            pltpu.VMEM((H, S, R, dh), BF16),
            pltpu.SemaphoreType.DMA((H, S, 3)),
            pltpu.SemaphoreType.DMA((H, S)),
            pltpu.SemaphoreType.DMA((H, G)),
            pltpu.SemaphoreType.DMA((H, G)),
            pltpu.SemaphoreType.DMA((H, G)),
            pltpu.SemaphoreType.DMA((H, G)),
            pltpu.SemaphoreType.DMA((H, S)),
            pltpu.SemaphoreType.DMA((H, S)),
        ],
        compiler_params=pltpu.CompilerParams(
            collective_id=0, has_side_effects=True, vmem_limit_bytes=52 * 1024 * 1024
        ),
        cost_estimate=pl.CostEstimate(
            flops=4 * pairs * dh, bytes_accessed=2 * H * S * R * W, transcendentals=pairs
        ),
    )(x, code, bias)


def expert_kernel(
    S, G, GC, SC, NQ, Dc,
    normed_ref, mixed_ref, match_ref, share_ref, perm_ref, wg_hbm, wu_hbm, wd_hbm, out_ref,
    zsel, zin, psend, parr, rsend, rarr, zout, zfin, wg, wu, wd, gate_acc, up_acc,
    zs_send, zs_recv, ps_send, ps_recv, rs_send, rs_recv, bs_send, bs_recv, w_sem,
):
    s = lax.axis_index("seq")
    g = lax.axis_index("grp")
    rows = G * SC

    loads = [
        pltpu.make_async_copy(wg_hbm, wg, w_sem.at[0]),
        pltpu.make_async_copy(wu_hbm, wu, w_sem.at[1]),
        pltpu.make_async_copy(wd_hbm, wd, w_sem.at[2]),
    ]
    barrier = pltpu.get_barrier_semaphore()
    for d in range(1, S):
        pl.semaphore_signal(barrier, inc=1, device_id=(lax.rem(s + d, S), g), device_id_type=MESH)
    for d in range(1, G):
        pl.semaphore_signal(barrier, inc=1, device_id=(s, lax.rem(g + d, G)), device_id_type=MESH)

    def along_seq(source, target, send, recv):
        def copy(q, d):
            to = lax.rem(s + d, S)
            return pltpu.make_async_remote_copy(
                src_ref=source.at[q, to], dst_ref=target.at[q, s],
                send_sem=send.at[q, d], recv_sem=recv.at[q, s],
                device_id=(to, g), device_id_type=MESH,
            )

        def start(q):
            for d in range(1, S):
                copy(q, d).start()
            pltpu.make_async_copy(source.at[q, s], target.at[q, s], recv.at[q, s]).start()

        def arrive(q):
            for y in range(S):
                pltpu.make_async_copy(target.at[q, y], target.at[q, y], recv.at[q, y]).wait()

        def sent(q):
            for d in range(1, S):
                copy(q, d).wait_send()

        return start, arrive, sent

    def along_grp(source, target, send, recv):
        def copy(q, d):
            to = lax.rem(g + d, G)
            return pltpu.make_async_remote_copy(
                src_ref=source.at[q, to], dst_ref=target.at[q, g],
                send_sem=send.at[q, d], recv_sem=recv.at[q, g],
                device_id=(s, to), device_id_type=MESH,
            )

        def start(q):
            for d in range(1, G):
                copy(q, d).start()
            pltpu.make_async_copy(source.at[q, g], target.at[q, g], recv.at[q, g]).start()

        def arrive(q):
            for y in range(G):
                pltpu.make_async_copy(target.at[q, y], target.at[q, y], recv.at[q, y]).wait()

        def sent(q):
            for d in range(1, G):
                copy(q, d).wait_send()

        return start, arrive, sent

    z_start, z_arrive, z_sent = along_seq(zsel, zin, zs_send, zs_recv)
    p_start, p_arrive, p_sent = along_grp(psend, parr, ps_send, ps_recv)
    r_start, r_arrive, r_sent = along_grp(rsend, rarr, rs_send, rs_recv)
    b_start, b_arrive, b_sent = along_seq(zout, zfin, bs_send, bs_recv)

    def columns(q):
        return pl.ds(pl.multiple_of(q * Dc, Dc), Dc)

    def select(q):
        picked = jnp.dot(match_ref[...], normed_ref[:, columns(q)], preferred_element_type=F32)
        zsel[q] = picked.astype(BF16).reshape(S, GC, Dc)

    select(0)
    if NQ > 1:
        select(1)
    pl.semaphore_wait(barrier, S + G - 2)
    z_start(0)
    if NQ > 1:
        z_start(1)
    for load in loads:
        load.start()
    gate_acc[...] = jnp.zeros_like(gate_acc)
    up_acc[...] = jnp.zeros_like(up_acc)

    @pl.loop(2, NQ)
    def _(q):
        select(q)

    for load in loads:
        load.wait()

    @pl.loop(0, NQ + 1)
    def _(t):
        @pl.when(t < NQ)
        def _():
            z_arrive(t)

            @pl.when(t + 2 < NQ)
            def _():
                z_start(t + 2)

            moved = jnp.dot(
                perm_ref[...], zin[t].reshape(rows, Dc), preferred_element_type=F32
            )
            psend[t] = moved.astype(BF16).reshape(G, SC, Dc)
            p_start(t)

        @pl.when(t >= 1)
        def _():
            q = t - 1
            p_arrive(q)
            taken = parr[q].reshape(rows, Dc)
            gate_acc[...] += jnp.dot(taken, wg[columns(q), :], preferred_element_type=F32)
            up_acc[...] += jnp.dot(taken, wu[columns(q), :], preferred_element_type=F32)

    gate = gate_acc[...]
    hidden = (gate * jax.nn.sigmoid(gate) * up_acc[...]).astype(BF16)

    for q in range(NQ):
        result = jnp.dot(hidden, wd[:, q * Dc : (q + 1) * Dc], preferred_element_type=F32)
        rsend[q] = result.astype(BF16).reshape(G, SC, Dc)
        r_start(q)

    @pl.loop(0, NQ + 2)
    def _(t):
        @pl.when(t < NQ)
        def _():
            r_arrive(t)
            moved = lax.dot_general(
                perm_ref[...], rarr[t].reshape(rows, Dc), (((0,), (0,)), ((), ())),
                preferred_element_type=F32,
            )
            zout[t] = moved.astype(BF16).reshape(S, GC, Dc)
            b_start(t)

        @pl.when(t >= 2)
        def _():
            q = t - 2
            b_arrive(q)
            total = jnp.dot(
                share_ref[...], zfin[q].reshape(rows, Dc), preferred_element_type=F32
            )
            out_ref[:, columns(q)] = (mixed_ref[:, columns(q)].astype(F32) + total).astype(BF16)

    @pl.loop(0, NQ)
    def _(q):
        z_sent(q)
        p_sent(q)
        r_sent(q)
        b_sent(q)


def run_experts(normed, mixed, match, share, perm, wg, wu, wd, S, G, cap):
    R, D = normed.shape
    hidden = wg.shape[1]
    NQ = 8
    Dc = D // NQ
    GC, SC = G * cap, S * cap
    rows = S * GC
    vmem = pl.BlockSpec(memory_space=pltpu.VMEM)
    hbm = pl.BlockSpec(memory_space=pl.ANY)
    by_seq = pltpu.VMEM((NQ, S, GC, Dc), BF16)
    by_grp = pltpu.VMEM((NQ, G, SC, Dc), BF16)
    seq_sem = pltpu.SemaphoreType.DMA((NQ, S))
    grp_sem = pltpu.SemaphoreType.DMA((NQ, G))
    return pl.pallas_call(
        functools.partial(expert_kernel, S, G, GC, SC, NQ, Dc),
        out_shape=jax.ShapeDtypeStruct((R, D), BF16),
        in_specs=[vmem, vmem, vmem, vmem, vmem, hbm, hbm, hbm],
        out_specs=vmem,
        scratch_shapes=[
            by_seq, by_seq, by_grp, by_grp, by_grp, by_grp, by_seq, by_seq,
            pltpu.VMEM((D, hidden), BF16),
            pltpu.VMEM((D, hidden), BF16),
            pltpu.VMEM((hidden, D), BF16),
            pltpu.VMEM((rows, hidden), F32),
            pltpu.VMEM((rows, hidden), F32),
            seq_sem, seq_sem, grp_sem, grp_sem, grp_sem, grp_sem, seq_sem, seq_sem,
            pltpu.SemaphoreType.DMA((3,)),
        ],
        compiler_params=pltpu.CompilerParams(
            collective_id=1, has_side_effects=True, vmem_limit_bytes=60 * 1024 * 1024
        ),
        cost_estimate=pl.CostEstimate(
            flops=6 * rows * D * hidden, bytes_accessed=6 * D * hidden, transcendentals=rows * hidden
        ),
    )(normed, mixed, match, share, perm, wg, wu, wd)


def slot_codes(mask):
    rows = mask.shape[-1]
    before = jnp.triu(jnp.ones((rows, rows), BF16), 1)
    ranks = jnp.einsum("...r,rq->...q", mask.astype(BF16), before, preferred_element_type=F32)
    return jnp.where(mask > 0, ranks, -1.0)


def shards(qkv, cluster_lists, w_out, norm_gain, router, expert_lists, w_gate, w_up, w_down):
    R = qkv.shape[0]
    S = lax.axis_size("seq")
    G = lax.axis_size("grp")
    devices = S * G
    H = cluster_lists.shape[0]
    dh = qkv.shape[2] // (H * S)
    my_index = lax.axis_index("seq") * G + lax.axis_index("grp")
    C = round_up(3 * (R // G) // 2, 16)

    x = qkv.reshape(R, 3 * S * H * dh)
    members = cluster_lists[:, 0, :]
    lanes = 128
    high = (
        (members // lanes)[:, None, :] == jnp.arange(devices * R // lanes, dtype=jnp.int32)[:, None]
    )
    low = (members % lanes)[:, :, None] == jnp.arange(lanes, dtype=jnp.int32)
    mask = jnp.einsum(
        "hip,hpl->hil", high.astype(BF16), low.astype(BF16), preferred_element_type=F32
    ).reshape(H, S, G, R)
    counts = jnp.sum(mask, axis=3)
    slots = jnp.arange(C, dtype=F32)
    bias = jnp.where(slots < counts[..., None], 0.0, -1e30).reshape(H, S, 1, G * C)
    asked = lax.all_to_all(mask.astype(BF16), "grp", split_axis=2, concat_axis=2, tiled=True)
    code = slot_codes(asked)

    attended = cluster_attention(x, code, bias, S, G, H, R, C, dh)
    mixed = jnp.dot(attended, w_out, preferred_element_type=F32).astype(BF16)
    wide = mixed.astype(F32)
    mean_square = jnp.mean(wide * wide, axis=1, keepdims=True)
    normed = (wide * lax.rsqrt(mean_square + 1e-06) * norm_gain.astype(F32)).astype(BF16)
    gates = jax.nn.sigmoid(jnp.dot(normed, router, preferred_element_type=F32))

    E, chosen_len = expert_lists.shape
    cap = 3 * (chosen_len // devices) // 2
    row_iota = jnp.arange(R, dtype=jnp.int32)
    here = expert_lists - my_index * R
    expert_mask = jnp.sum((here[:, :, None] == row_iota).astype(F32), axis=1)
    expert_code = slot_codes(expert_mask)
    match = expert_code[:, None, :] == jnp.arange(cap, dtype=F32)[None, :, None]
    share = jnp.where(match, gates.T[:, None, :], 0.0).astype(BF16).reshape(E * cap, R).T
    match = match.astype(BF16).reshape(E * cap, R)
    place = jnp.arange(E * cap, dtype=jnp.int32)
    by_seq = place.reshape(S, G, cap).transpose(1, 0, 2).reshape(-1)
    perm = (by_seq[:, None] == place[None, :]).astype(BF16)
    return run_experts(
        normed, mixed, match, share, perm, w_gate[0], w_up[0], w_down[0], S, G, cap
    )


def solution(mesh):
    return jax.shard_map(
        shards,
        mesh=mesh,
        in_specs=(
            P(("seq", "grp"), None, None),
            P("seq", "grp", None),
            P(),
            P(),
            P(),
            P(),
            P(("seq", "grp"), None, None),
            P(("seq", "grp"), None, None),
            P(("seq", "grp"), None, None),
        ),
        out_specs=P(("seq", "grp"), None),
        check_vma=False,
    )
```

```python
import functools

import jax
import jax.numpy as jnp
from jax import lax
from jax.experimental import pallas as pl
from jax.experimental.pallas import tpu as pltpu
from jax.sharding import PartitionSpec as P

MESH = pl.DeviceIdType.MESH
F32 = jnp.float32
BF16 = jnp.bfloat16


def round_up(value, step):
    return (value + step - 1) // step * step


def select_matrix(code, slots):
    lists, rows = code.shape
    slot_iota = lax.broadcasted_iota(jnp.int32, (slots, rows), 0).astype(F32)
    parts = [
        jnp.where(code[g : g + 1, :] == slot_iota, 1.0, 0.0).astype(BF16) for g in range(lists)
    ]
    return jnp.concatenate(parts, axis=0)


def attention_kernel(
    S, G, H, R, C, dh, scale,
    x_ref, code_ref, bias_ref, out_ref,
    zin, psend, arr, osend, oarr, zback,
    zs_send, zs_recv, ps_send, ps_recv, os_send, os_recv, bs_send, bs_recv,
):
    s = lax.axis_index("seq")
    g = lax.axis_index("grp")

    barrier = pltpu.get_barrier_semaphore()
    for d in range(1, S):
        pl.semaphore_signal(barrier, inc=1, device_id=(lax.rem(s + d, S), g), device_id_type=MESH)
    for d in range(1, G):
        pl.semaphore_signal(barrier, inc=1, device_id=(s, lax.rem(g + d, G)), device_id_type=MESH)
    pl.semaphore_wait(barrier, S + G - 2)

    def head_part(owner, j, k):
        return x_ref.at[:, pl.ds(pl.multiple_of(((k * S + owner) * H + j) * dh, dh), dh)]

    def z_copy(j, d, k):
        to = lax.rem(s + d, S)
        return pltpu.make_async_remote_copy(
            src_ref=head_part(to, j, k), dst_ref=zin.at[j, s, :, k * dh : (k + 1) * dh],
            send_sem=zs_send.at[j, d, k], recv_sem=zs_recv.at[j, s],
            device_id=(to, g), device_id_type=MESH,
        )

    def z_own(j, k):
        return pltpu.make_async_copy(
            head_part(s, j, k), zin.at[j, s, :, k * dh : (k + 1) * dh], zs_recv.at[j, s]
        )

    def z_arrival(j, src):
        return pltpu.make_async_copy(zin.at[j, src], zin.at[j, src], zs_recv.at[j, src])

    def p_copy(j, d):
        to = lax.rem(g + d, G)
        return pltpu.make_async_remote_copy(
            src_ref=psend.at[j, :, to], dst_ref=arr.at[j, :, g],
            send_sem=ps_send.at[j, d], recv_sem=ps_recv.at[j, g],
            device_id=(s, to), device_id_type=MESH,
        )

    def p_own(j):
        return pltpu.make_async_copy(psend.at[j, :, g], arr.at[j, :, g], ps_recv.at[j, g])

    def p_arrival(j, src):
        return pltpu.make_async_copy(arr.at[j, :, src], arr.at[j, :, src], ps_recv.at[j, src])

    def o_copy(j, d):
        to = lax.rem(g + d, G)
        return pltpu.make_async_remote_copy(
            src_ref=osend.at[j, :, to], dst_ref=oarr.at[j, :, g],
            send_sem=os_send.at[j, d], recv_sem=os_recv.at[j, g],
            device_id=(s, to), device_id_type=MESH,
        )

    def o_own(j):
        return pltpu.make_async_copy(osend.at[j, :, g], oarr.at[j, :, g], os_recv.at[j, g])

    def o_arrival(j, src):
        return pltpu.make_async_copy(oarr.at[j, :, src], oarr.at[j, :, src], os_recv.at[j, src])

    def columns(owner, j):
        return pl.ds(pl.multiple_of((owner * H + j) * dh, dh), dh)

    def b_copy(j, d):
        to = lax.rem(s + d, S)
        return pltpu.make_async_remote_copy(
            src_ref=zback.at[j, to], dst_ref=out_ref.at[:, columns(s, j)],
            send_sem=bs_send.at[j, d], recv_sem=bs_recv.at[j, s],
            device_id=(to, g), device_id_type=MESH,
        )

    def b_own(j):
        return pltpu.make_async_copy(
            zback.at[j, s], out_ref.at[:, columns(s, j)], bs_recv.at[j, s]
        )

    def b_arrival(j, src):
        where = out_ref.at[:, columns(src, j)]
        return pltpu.make_async_copy(where, where, bs_recv.at[j, src])

    def z_start(j):
        for k in range(3):
            for d in range(1, S):
                z_copy(j, d, k).start()
            z_own(j, k).start()

    z_start(0)
    if H > 1:
        z_start(1)

    def route(j):
        for src in range(S):
            z_arrival(j, src).wait()

        @pl.when(j + 2 < H)
        def _():
            z_start(j + 2)

        for z in range(S):
            sel = select_matrix(code_ref[j, z], C)
            picked = jnp.dot(sel, zin[j, z], preferred_element_type=F32)
            psend[j, z] = picked.astype(BF16).reshape(G, C, 3 * dh)
        for d in range(1, G):
            p_copy(j, d).start()
        p_own(j).start()

    def attend(j):
        for src in range(G):
            p_arrival(j, src).wait()
        n = G * C
        causal = lax.broadcasted_iota(jnp.int32, (n, n), 0) >= lax.broadcasted_iota(
            jnp.int32, (n, n), 1
        )
        for z in range(S):
            q = arr[j, z, :, :, 0:dh].reshape(n, dh)
            scores = []
            for y in range(z + 1):
                k = arr[j, y, :, :, dh : 2 * dh].reshape(n, dh)
                part = lax.dot_general(
                    q, k, (((1,), (1,)), ((), ())), preferred_element_type=F32
                )
                part = part * scale + bias_ref[j, y]
                if y == z:
                    part = jnp.where(causal, part, -1e30)
                scores.append(part)
            top = functools.reduce(
                jnp.maximum, [jnp.max(part, axis=1, keepdims=True) for part in scores]
            )
            total = jnp.zeros((n, 1), F32)
            acc = jnp.zeros((n, dh), F32)
            for y in range(z + 1):
                e = jnp.exp(scores[y] - top)
                total = total + jnp.sum(e, axis=1, keepdims=True)
                v = arr[j, y, :, :, 2 * dh : 3 * dh].reshape(n, dh)
                acc = acc + jnp.dot(e.astype(BF16), v, preferred_element_type=F32)
            osend[j, z] = (acc / total).astype(BF16).reshape(G, C, dh)
        for d in range(1, G):
            o_copy(j, d).start()
        o_own(j).start()

    def give_back(j):
        for src in range(G):
            o_arrival(j, src).wait()
        for z in range(S):
            sel = select_matrix(code_ref[j, z], C)
            rows = lax.dot_general(
                sel, oarr[j, z].reshape(G * C, dh), (((0,), (0,)), ((), ())),
                preferred_element_type=F32,
            )
            zback[j, z] = rows.astype(BF16)
        for d in range(1, S):
            b_copy(j, d).start()
        b_own(j).start()

    @pl.loop(0, H + 2)
    def _(t):
        @pl.when(t < H)
        def _():
            route(t)

        @pl.when((t >= 1) & (t <= H))
        def _():
            attend(t - 1)

        @pl.when(t >= 2)
        def _():
            give_back(t - 2)

    @pl.loop(0, H)
    def _(j):
        for src in range(S):
            b_arrival(j, src).wait()
        for d in range(1, S):
            for k in range(3):
                z_copy(j, d, k).wait_send()
            b_copy(j, d).wait_send()
        for d in range(1, G):
            p_copy(j, d).wait_send()
            o_copy(j, d).wait_send()


def cluster_attention(x, code, bias, S, G, H, R, C, dh):
    W = 3 * dh
    vmem = pl.BlockSpec(memory_space=pltpu.VMEM)
    pairs = H * S * G * C * G * C * (S + 1) // 2
    return pl.pallas_call(
        functools.partial(attention_kernel, S, G, H, R, C, dh, dh ** (-0.5)),
        out_shape=jax.ShapeDtypeStruct((R, S * H * dh), BF16),
        in_specs=[pl.BlockSpec(memory_space=pl.ANY), vmem, vmem],
        out_specs=vmem,
        scratch_shapes=[
            pltpu.VMEM((H, S, R, W), BF16),
            pltpu.VMEM((H, S, G, C, W), BF16),
            pltpu.VMEM((H, S, G, C, W), BF16),
            pltpu.VMEM((H, S, G, C, dh), BF16),
            pltpu.VMEM((H, S, G, C, dh), BF16),
            pltpu.VMEM((H, S, R, dh), BF16),
            pltpu.SemaphoreType.DMA((H, S, 3)),
            pltpu.SemaphoreType.DMA((H, S)),
            pltpu.SemaphoreType.DMA((H, G)),
            pltpu.SemaphoreType.DMA((H, G)),
            pltpu.SemaphoreType.DMA((H, G)),
            pltpu.SemaphoreType.DMA((H, G)),
            pltpu.SemaphoreType.DMA((H, S)),
            pltpu.SemaphoreType.DMA((H, S)),
        ],
        compiler_params=pltpu.CompilerParams(
            collective_id=0, has_side_effects=True, vmem_limit_bytes=52 * 1024 * 1024
        ),
        cost_estimate=pl.CostEstimate(
            flops=4 * pairs * dh, bytes_accessed=2 * H * S * R * W, transcendentals=pairs
        ),
    )(x, code, bias)


def expert_kernel(
    S, G, GC, SC, NQ, Dc,
    normed_ref, mixed_ref, match_ref, share_ref, perm_ref, wg_hbm, wu_hbm, wd_hbm, out_ref,
    zsel, zin, psend, parr, rsend, rarr, zout, zfin, wg, wu, wd, gate_acc, up_acc,
    zs_send, zs_recv, ps_send, ps_recv, rs_send, rs_recv, bs_send, bs_recv, w_sem,
):
    s = lax.axis_index("seq")
    g = lax.axis_index("grp")
    rows = G * SC

    loads = [
        pltpu.make_async_copy(wg_hbm, wg, w_sem.at[0]),
        pltpu.make_async_copy(wu_hbm, wu, w_sem.at[1]),
        pltpu.make_async_copy(wd_hbm, wd, w_sem.at[2]),
    ]
    barrier = pltpu.get_barrier_semaphore()
    for d in range(1, S):
        pl.semaphore_signal(barrier, inc=1, device_id=(lax.rem(s + d, S), g), device_id_type=MESH)
    for d in range(1, G):
        pl.semaphore_signal(barrier, inc=1, device_id=(s, lax.rem(g + d, G)), device_id_type=MESH)

    def along_seq(source, target, send, recv):
        def copy(q, d):
            to = lax.rem(s + d, S)
            return pltpu.make_async_remote_copy(
                src_ref=source.at[q, to], dst_ref=target.at[q, s],
                send_sem=send.at[q, d], recv_sem=recv.at[q, s],
                device_id=(to, g), device_id_type=MESH,
            )

        def start(q):
            for d in range(1, S):
                copy(q, d).start()
            pltpu.make_async_copy(source.at[q, s], target.at[q, s], recv.at[q, s]).start()

        def arrive(q):
            for y in range(S):
                pltpu.make_async_copy(target.at[q, y], target.at[q, y], recv.at[q, y]).wait()

        def sent(q):
            for d in range(1, S):
                copy(q, d).wait_send()

        return start, arrive, sent

    def along_grp(source, target, send, recv):
        def copy(q, d):
            to = lax.rem(g + d, G)
            return pltpu.make_async_remote_copy(
                src_ref=source.at[q, to], dst_ref=target.at[q, g],
                send_sem=send.at[q, d], recv_sem=recv.at[q, g],
                device_id=(s, to), device_id_type=MESH,
            )

        def start(q):
            for d in range(1, G):
                copy(q, d).start()
            pltpu.make_async_copy(source.at[q, g], target.at[q, g], recv.at[q, g]).start()

        def arrive(q):
            for y in range(G):
                pltpu.make_async_copy(target.at[q, y], target.at[q, y], recv.at[q, y]).wait()

        def sent(q):
            for d in range(1, G):
                copy(q, d).wait_send()

        return start, arrive, sent

    z_start, z_arrive, z_sent = along_seq(zsel, zin, zs_send, zs_recv)
    p_start, p_arrive, p_sent = along_grp(psend, parr, ps_send, ps_recv)
    r_start, r_arrive, r_sent = along_grp(rsend, rarr, rs_send, rs_recv)
    b_start, b_arrive, b_sent = along_seq(zout, zfin, bs_send, bs_recv)

    def columns(q):
        return pl.ds(pl.multiple_of(q * Dc, Dc), Dc)

    def select(q):
        picked = jnp.dot(match_ref[...], normed_ref[:, columns(q)], preferred_element_type=F32)
        zsel[q] = picked.astype(BF16).reshape(S, GC, Dc)

    select(0)
    if NQ > 1:
        select(1)
    pl.semaphore_wait(barrier, S + G - 2)
    z_start(0)
    if NQ > 1:
        z_start(1)
    for load in loads:
        load.start()
    gate_acc[...] = jnp.zeros_like(gate_acc)
    up_acc[...] = jnp.zeros_like(up_acc)

    @pl.loop(2, NQ)
    def _(q):
        select(q)

    for load in loads:
        load.wait()

    @pl.loop(0, NQ + 1)
    def _(t):
        @pl.when(t < NQ)
        def _():
            z_arrive(t)

            @pl.when(t + 2 < NQ)
            def _():
                z_start(t + 2)

            moved = jnp.dot(
                perm_ref[...], zin[t].reshape(rows, Dc), preferred_element_type=F32
            )
            psend[t] = moved.astype(BF16).reshape(G, SC, Dc)
            p_start(t)

        @pl.when(t >= 1)
        def _():
            q = t - 1
            p_arrive(q)
            taken = parr[q].reshape(rows, Dc)
            gate_acc[...] += jnp.dot(taken, wg[columns(q), :], preferred_element_type=F32)
            up_acc[...] += jnp.dot(taken, wu[columns(q), :], preferred_element_type=F32)

    gate = gate_acc[...]
    hidden = (gate * jax.nn.sigmoid(gate) * up_acc[...]).astype(BF16)

    for q in range(NQ):
        result = jnp.dot(hidden, wd[:, q * Dc : (q + 1) * Dc], preferred_element_type=F32)
        rsend[q] = result.astype(BF16).reshape(G, SC, Dc)
        r_start(q)

    @pl.loop(0, NQ + 2)
    def _(t):
        @pl.when(t < NQ)
        def _():
            r_arrive(t)
            moved = lax.dot_general(
                perm_ref[...], rarr[t].reshape(rows, Dc), (((0,), (0,)), ((), ())),
                preferred_element_type=F32,
            )
            zout[t] = moved.astype(BF16).reshape(S, GC, Dc)
            b_start(t)

        @pl.when(t >= 2)
        def _():
            q = t - 2
            b_arrive(q)
            total = jnp.dot(
                share_ref[...], zfin[q].reshape(rows, Dc), preferred_element_type=F32
            )
            out_ref[:, columns(q)] = (mixed_ref[:, columns(q)].astype(F32) + total).astype(BF16)

    @pl.loop(0, NQ)
    def _(q):
        z_sent(q)
        p_sent(q)
        r_sent(q)
        b_sent(q)


def run_experts(normed, mixed, match, share, perm, wg, wu, wd, S, G, cap):
    R, D = normed.shape
    hidden = wg.shape[1]
    NQ = 8
    Dc = D // NQ
    GC, SC = G * cap, S * cap
    rows = S * GC
    vmem = pl.BlockSpec(memory_space=pltpu.VMEM)
    hbm = pl.BlockSpec(memory_space=pl.ANY)
    by_seq = pltpu.VMEM((NQ, S, GC, Dc), BF16)
    by_grp = pltpu.VMEM((NQ, G, SC, Dc), BF16)
    seq_sem = pltpu.SemaphoreType.DMA((NQ, S))
    grp_sem = pltpu.SemaphoreType.DMA((NQ, G))
    return pl.pallas_call(
        functools.partial(expert_kernel, S, G, GC, SC, NQ, Dc),
        out_shape=jax.ShapeDtypeStruct((R, D), BF16),
        in_specs=[vmem, vmem, vmem, vmem, vmem, hbm, hbm, hbm],
        out_specs=vmem,
        scratch_shapes=[
            by_seq, by_seq, by_grp, by_grp, by_grp, by_grp, by_seq, by_seq,
            pltpu.VMEM((D, hidden), BF16),
            pltpu.VMEM((D, hidden), BF16),
            pltpu.VMEM((hidden, D), BF16),
            pltpu.VMEM((rows, hidden), F32),
            pltpu.VMEM((rows, hidden), F32),
            seq_sem, seq_sem, grp_sem, grp_sem, grp_sem, grp_sem, seq_sem, seq_sem,
            pltpu.SemaphoreType.DMA((3,)),
        ],
        compiler_params=pltpu.CompilerParams(
            collective_id=1, has_side_effects=True, vmem_limit_bytes=60 * 1024 * 1024
        ),
        cost_estimate=pl.CostEstimate(
            flops=6 * rows * D * hidden, bytes_accessed=6 * D * hidden, transcendentals=rows * hidden
        ),
    )(normed, mixed, match, share, perm, wg, wu, wd)


def relay_kernel(
    S, G, GC, SC, NQ, Dc,
    normed_ref, mixed_ref, match_ref, share_ref, perm_ref, far_ref, router_ref,
    wg_hbm, wu_hbm, wd_hbm, out_ref,
    zsel, zin, psend, parr, rsend, rarr, zout, zfin, wg, wu, wd, gate_acc, up_acc,
    dense, hsel, rel, dout, dfin, logits, far_share,
    ps_send, ps_recv, rs_send, rs_recv, zs_send, zs_recv, bs_send, bs_recv,
    d_send, d_recv, h_send, l_send, l_recv, f_send, f_recv, w_sem,
):
    s = lax.axis_index("seq")
    g = lax.axis_index("grp")
    rows = G * SC

    loads = [
        pltpu.make_async_copy(wg_hbm, wg, w_sem.at[0]),
        pltpu.make_async_copy(wu_hbm, wu, w_sem.at[1]),
        pltpu.make_async_copy(wd_hbm, wd, w_sem.at[2]),
    ]
    barrier = pltpu.get_barrier_semaphore()
    for d in range(1, S):
        pl.semaphore_signal(barrier, inc=1, device_id=(lax.rem(s + d, S), g), device_id_type=MESH)
    for d in range(1, G):
        pl.semaphore_signal(barrier, inc=1, device_id=(s, lax.rem(g + d, G)), device_id_type=MESH)

    side = s // 2
    spot = s - 2 * side
    mate = 2 * side + 1 - spot
    far_first = 2 - 2 * side
    far_relay = 2 - side
    relay = (s == 1) | (s == 2)

    def remote(source, target, send, recv, to):
        return pltpu.make_async_remote_copy(
            src_ref=source, dst_ref=target, send_sem=send, recv_sem=recv,
            device_id=(to, g), device_id_type=MESH,
        )

    def arrived(ref, sem):
        pltpu.make_async_copy(ref, ref, sem).wait()

    def near_copy(q):
        return remote(
            zsel.at[q, 1 - spot], zin.at[q, s], zs_send.at[q], zs_recv.at[q, s], mate
        )

    def dense_copy(q):
        return remote(
            normed_ref.at[:, columns(q)], dense.at[q, spot], d_send.at[q], d_recv.at[q, spot],
            far_relay,
        )

    def hop_copy(q, i):
        y = far_first + i
        return remote(
            hsel.at[q, i, 1 - spot], zin.at[q, y], h_send.at[q, i], zs_recv.at[q, y], mate
        )

    def z_start(q):
        dense_copy(q).start()
        near_copy(q).start()
        pltpu.make_async_copy(zsel.at[q, spot], zin.at[q, s], zs_recv.at[q, s]).start()

    def z_arrive(q):
        for y in range(S):
            arrived(zin.at[q, y], zs_recv.at[q, y])

    def relay_rows(q):
        for i in range(2):
            y = far_first + i
            arrived(dense.at[q, i], d_recv.at[q, i])
            picked = jnp.dot(far_ref[i], dense[q, i], preferred_element_type=F32)
            hsel[q, i] = picked.astype(BF16).reshape(2, GC, Dc)
            hop_copy(q, i).start()
            pltpu.make_async_copy(hsel.at[q, i, spot], zin.at[q, y], zs_recv.at[q, y]).start()
            logits[i] += lax.dot_general(
                router_ref[:, columns(q)], dense[q, i], (((1,), (1,)), ((), ())),
                preferred_element_type=F32,
            )

    def near_back(q):
        return remote(
            zout.at[q, mate], zfin.at[q, spot], bs_send.at[q], bs_recv.at[q, spot], mate
        )

    def lend_copy(q, i):
        return remote(
            zout.at[q, far_first + i], rel.at[q, i], l_send.at[q, i], l_recv.at[q, i], mate
        )

    def far_copy(q, i):
        return remote(
            dout.at[q, i], dfin.at[q], f_send.at[q, i], f_recv.at[q], far_first + i
        )

    def b_start(q):
        @pl.when(jnp.logical_not(relay))
        def _():
            for i in range(2):
                lend_copy(q, i).start()

        near_back(q).start()
        pltpu.make_async_copy(zout.at[q, s], zfin.at[q, spot], bs_recv.at[q, spot]).start()

    def relay_results(q):
        for i in range(2):
            arrived(rel.at[q, i], l_recv.at[q, i])
            mine = lax.dot_general(
                far_share[i, spot], zout[q, far_first + i], (((0,), (0,)), ((), ())),
                preferred_element_type=F32,
            )
            theirs = lax.dot_general(
                far_share[i, 1 - spot], rel[q, i], (((0,), (0,)), ((), ())),
                preferred_element_type=F32,
            )
            dout[q, i] = (mine + theirs).astype(BF16)
            far_copy(q, i).start()

    def b_arrive(q):
        for i in range(2):
            arrived(zfin.at[q, i], bs_recv.at[q, i])
        arrived(dfin.at[q], f_recv.at[q])

    def along_grp(source, target, send, recv):
        def copy(q, d):
            to = lax.rem(g + d, G)
            return pltpu.make_async_remote_copy(
                src_ref=source.at[q, to], dst_ref=target.at[q, g],
                send_sem=send.at[q, d], recv_sem=recv.at[q, g],
                device_id=(s, to), device_id_type=MESH,
            )

        def start(q):
            for d in range(1, G):
                copy(q, d).start()
            pltpu.make_async_copy(source.at[q, g], target.at[q, g], recv.at[q, g]).start()

        def arrive(q):
            for y in range(G):
                pltpu.make_async_copy(target.at[q, y], target.at[q, y], recv.at[q, y]).wait()

        def sent(q):
            for d in range(1, G):
                copy(q, d).wait_send()

        return start, arrive, sent

    p_start, p_arrive, p_sent = along_grp(psend, parr, ps_send, ps_recv)
    r_start, r_arrive, r_sent = along_grp(rsend, rarr, rs_send, rs_recv)

    def columns(q):
        return pl.ds(pl.multiple_of(q * Dc, Dc), Dc)

    def select(q):
        picked = jnp.dot(match_ref[...], normed_ref[:, columns(q)], preferred_element_type=F32)
        zsel[q] = picked.astype(BF16).reshape(2, GC, Dc)

    logits[...] = jnp.zeros_like(logits)
    select(0)
    if NQ > 1:
        select(1)
    pl.semaphore_wait(barrier, S + G - 2)
    z_start(0)
    if NQ > 1:
        z_start(1)
    for load in loads:
        load.start()
    gate_acc[...] = jnp.zeros_like(gate_acc)
    up_acc[...] = jnp.zeros_like(up_acc)

    @pl.loop(2, NQ)
    def _(q):
        select(q)

        @pl.when(q < 4)
        def _():
            z_start(q)

    for load in loads:
        load.wait()

    @pl.loop(0, NQ + 1)
    def _(t):
        @pl.when(t < NQ)
        def _():
            @pl.when(relay)
            def _():
                relay_rows(t)

            z_arrive(t)

            @pl.when(t + 4 < NQ)
            def _():
                z_start(t + 4)

            moved = jnp.dot(
                perm_ref[...], zin[t].reshape(rows, Dc), preferred_element_type=F32
            )
            psend[t] = moved.astype(BF16).reshape(G, SC, Dc)
            p_start(t)

        @pl.when(t >= 1)
        def _():
            q = t - 1
            p_arrive(q)
            taken = parr[q].reshape(rows, Dc)
            gate_acc[...] += jnp.dot(taken, wg[columns(q), :], preferred_element_type=F32)
            up_acc[...] += jnp.dot(taken, wu[columns(q), :], preferred_element_type=F32)

    gate = gate_acc[...]
    hidden = (gate * jax.nn.sigmoid(gate) * up_acc[...]).astype(BF16)

    for q in range(NQ):
        result = jnp.dot(hidden, wd[:, q * Dc : (q + 1) * Dc], preferred_element_type=F32)
        rsend[q] = result.astype(BF16).reshape(G, SC, Dc)
        r_start(q)

    @pl.when(relay)
    def _():
        for i in range(2):
            weighted = far_ref[i].astype(F32) * jax.nn.sigmoid(logits[i])
            far_share[i] = weighted.astype(BF16).reshape(2, GC, weighted.shape[1])

    @pl.loop(0, NQ + 4)
    def _(t):
        @pl.when(t < NQ)
        def _():
            r_arrive(t)
            moved = lax.dot_general(
                perm_ref[...], rarr[t].reshape(rows, Dc), (((0,), (0,)), ((), ())),
                preferred_element_type=F32,
            )
            zout[t] = moved.astype(BF16).reshape(S, GC, Dc)
            b_start(t)

        @pl.when((t >= 1) & (t <= NQ) & relay)
        def _():
            relay_results(t - 1)

        @pl.when(t >= 4)
        def _():
            q = t - 4
            b_arrive(q)
            total = jnp.dot(
                share_ref[...], zfin[q].reshape(2 * GC, Dc), preferred_element_type=F32
            )
            total = total + dfin[q].astype(F32)
            out_ref[:, columns(q)] = (mixed_ref[:, columns(q)].astype(F32) + total).astype(BF16)

    @pl.loop(0, NQ)
    def _(q):
        p_sent(q)
        r_sent(q)
        near_copy(q).wait_send()
        dense_copy(q).wait_send()
        near_back(q).wait_send()

        @pl.when(relay)
        def _():
            for i in range(2):
                hop_copy(q, i).wait_send()
                far_copy(q, i).wait_send()

        @pl.when(jnp.logical_not(relay))
        def _():
            for i in range(2):
                lend_copy(q, i).wait_send()


def run_relay(normed, mixed, match, share, perm, far, router, wg, wu, wd, S, G, cap):
    R, D = normed.shape
    hidden = wg.shape[1]
    NQ = 8
    Dc = D // NQ
    GC, SC = G * cap, S * cap
    rows = S * GC
    vmem = pl.BlockSpec(memory_space=pltpu.VMEM)
    hbm = pl.BlockSpec(memory_space=pl.ANY)
    by_seq = pltpu.VMEM((NQ, S, GC, Dc), BF16)
    pair = pltpu.VMEM((NQ, 2, GC, Dc), BF16)
    one_sem = pltpu.SemaphoreType.DMA((NQ,))
    two_sem = pltpu.SemaphoreType.DMA((NQ, 2))
    by_grp = pltpu.VMEM((NQ, G, SC, Dc), BF16)
    seq_sem = pltpu.SemaphoreType.DMA((NQ, S))
    grp_sem = pltpu.SemaphoreType.DMA((NQ, G))
    return pl.pallas_call(
        functools.partial(relay_kernel, S, G, GC, SC, NQ, Dc),
        out_shape=jax.ShapeDtypeStruct((R, D), BF16),
        in_specs=[vmem] * 7 + [hbm, hbm, hbm],
        out_specs=vmem,
        scratch_shapes=[
            pair, by_seq, by_grp, by_grp, by_grp, by_grp, by_seq, pair,
            pltpu.VMEM((D, hidden), BF16),
            pltpu.VMEM((D, hidden), BF16),
            pltpu.VMEM((hidden, D), BF16),
            pltpu.VMEM((rows, hidden), F32),
            pltpu.VMEM((rows, hidden), F32),
            pltpu.VMEM((NQ, 2, R, Dc), BF16),
            pltpu.VMEM((NQ, 2, 2, GC, Dc), BF16),
            pair,
            pltpu.VMEM((NQ, 2, R, Dc), BF16),
            pltpu.VMEM((NQ, R, Dc), BF16),
            pltpu.VMEM((2, 2 * GC, R), F32),
            pltpu.VMEM((2, 2, GC, R), BF16),
            grp_sem, grp_sem, grp_sem, grp_sem,
            one_sem, seq_sem, one_sem, two_sem,
            one_sem, two_sem, two_sem, two_sem, two_sem, two_sem, one_sem,
            pltpu.SemaphoreType.DMA((3,)),
        ],
        compiler_params=pltpu.CompilerParams(
            collective_id=2, has_side_effects=True, vmem_limit_bytes=60 * 1024 * 1024
        ),
        cost_estimate=pl.CostEstimate(
            flops=6 * rows * D * hidden, bytes_accessed=6 * D * hidden, transcendentals=rows * hidden
        ),
    )(normed, mixed, match, share, perm, far, router, wg, wu, wd)


def slot_codes(mask):
    rows = mask.shape[-1]
    before = jnp.triu(jnp.ones((rows, rows), BF16), 1)
    ranks = jnp.einsum("...r,rq->...q", mask.astype(BF16), before, preferred_element_type=F32)
    return jnp.where(mask > 0, ranks, -1.0)


def shards(qkv, cluster_lists, w_out, norm_gain, router, expert_lists, w_gate, w_up, w_down):
    R = qkv.shape[0]
    S = lax.axis_size("seq")
    G = lax.axis_size("grp")
    devices = S * G
    H = cluster_lists.shape[0]
    dh = qkv.shape[2] // (H * S)
    my_index = lax.axis_index("seq") * G + lax.axis_index("grp")
    C = round_up(3 * (R // G) // 2, 16)

    x = qkv.reshape(R, 3 * S * H * dh)
    members = cluster_lists[:, 0, :]
    lanes = 128
    high = (
        (members // lanes)[:, None, :] == jnp.arange(devices * R // lanes, dtype=jnp.int32)[:, None]
    )
    low = (members % lanes)[:, :, None] == jnp.arange(lanes, dtype=jnp.int32)
    mask = jnp.einsum(
        "hip,hpl->hil", high.astype(BF16), low.astype(BF16), preferred_element_type=F32
    ).reshape(H, S, G, R)
    counts = jnp.sum(mask, axis=3)
    slots = jnp.arange(C, dtype=F32)
    bias = jnp.where(slots < counts[..., None], 0.0, -1e30).reshape(H, S, 1, G * C)
    asked = lax.all_to_all(mask.astype(BF16), "grp", split_axis=2, concat_axis=2, tiled=True)
    code = slot_codes(asked)

    attended = cluster_attention(x, code, bias, S, G, H, R, C, dh)
    mixed = jnp.dot(attended, w_out, preferred_element_type=F32).astype(BF16)
    wide = mixed.astype(F32)
    mean_square = jnp.mean(wide * wide, axis=1, keepdims=True)
    normed = (wide * lax.rsqrt(mean_square + 1e-06) * norm_gain.astype(F32)).astype(BF16)
    gates = jax.nn.sigmoid(jnp.dot(normed, router, preferred_element_type=F32))

    E, chosen_len = expert_lists.shape
    cap = 3 * (chosen_len // devices) // 2
    row_iota = jnp.arange(R, dtype=jnp.int32)
    here = expert_lists - my_index * R
    expert_mask = jnp.sum((here[:, :, None] == row_iota).astype(F32), axis=1)
    expert_code = slot_codes(expert_mask)
    match = expert_code[:, None, :] == jnp.arange(cap, dtype=F32)[None, :, None]
    share = jnp.where(match, gates.T[:, None, :], 0.0).astype(BF16).reshape(E * cap, R).T
    match = match.astype(BF16).reshape(E * cap, R)
    place = jnp.arange(E * cap, dtype=jnp.int32)
    by_seq = place.reshape(S, G, cap).transpose(1, 0, 2).reshape(-1)
    perm = (by_seq[:, None] == place[None, :]).astype(BF16)
    if S == 4:
        side = lax.axis_index("seq") // 2
        half = E // 2
        near_lists = lax.dynamic_slice_in_dim(expert_lists, side * half, half, 0)
        far_block = (2 - 2 * side + jnp.arange(2, dtype=jnp.int32)) * G + lax.axis_index("grp")
        there = near_lists[None, :, :] - far_block[:, None, None] * R
        far_mask = jnp.sum((there[..., None] == row_iota).astype(F32), axis=2)
        far = slot_codes(far_mask)[:, :, None, :] == jnp.arange(cap, dtype=F32)[:, None]
        far = far.astype(BF16).reshape(2, half * cap, R)
        near_router = lax.dynamic_slice_in_dim(router.T, side * half, half, 0)
        near_router = jnp.repeat(near_router, cap, axis=0)
        near_match = lax.dynamic_slice_in_dim(match, side * half * cap, half * cap, 0)
        near_share = lax.dynamic_slice_in_dim(share, side * half * cap, half * cap, 1)
        return run_relay(
            normed, mixed, near_match, near_share, perm, far, near_router,
            w_gate[0], w_up[0], w_down[0], S, G, cap,
        )
    return run_experts(
        normed, mixed, match, share, perm, w_gate[0], w_up[0], w_down[0], S, G, cap
    )


def solution(mesh):
    return jax.shard_map(
        shards,
        mesh=mesh,
        in_specs=(
            P(("seq", "grp"), None, None),
            P("seq", "grp", None),
            P(),
            P(),
            P(),
            P(),
            P(("seq", "grp"), None, None),
            P(("seq", "grp"), None, None),
            P(("seq", "grp"), None, None),
        ),
        out_specs=P(("seq", "grp"), None),
        check_vma=False,
    )
```
